256 devices in a mesh: dp: 32 (over x, z), tensor: 8 (over y, core).
Axes of the slice: x: 4, y: 4, z: 8, core: 2. Of those that a mesh axis runs over, the one named last changes fastest.
Arguments:
- gradient: bfloat16 [2048, 28672], P('dp', 'tensor')
- owner: int32 [8, 4, 7], P('tensor'), may hold values from 0 to 31, as said below
- prev_left: float32 [8, 32, 512, 512], P('tensor', 'dp'), as said below
- prev_right: float32 [8, 32, 512, 512], P('tensor', 'dp'), as said below
Outputs:
- update: bfloat16 [2048, 28672], P('dp', 'tensor')
- stats_left: float32 [8, 32, 512, 512], P('tensor', 'dp')
- stats_right: float32 [8, 32, 512, 512], P('tensor', 'dp')
The draws below stay inside these ranges and needn't reach their ends.
Inputs may be any that keep to these rules, and one draw needn't show every extreme that they name: `owner`: in each tensor slice no dp index owns more than 1 block nor two blocks of the same row block i, and some dp index owns exactly 1. `prev_left`: symmetric positive definite. `prev_right`: symmetric positive definite.
All inputs are finite; a program needn't handle non-finite values.
Results may differ from the reference program's by a relative error of at most 0.0071.
Values may be sent and summed in bfloat16 or wider, within the bound.
No kernel may reach another device: no remote copies, remote signals or barrier semaphores. Data moves between devices by JAX's collectives and lax.ppermute only.
A program may use at most 64 MiB of HBM per device.

```python
import math
import jax
import jax.numpy as jnp
from jax import lax

BS = 512
CBT = 7
NRB = 4
CAP = 1
SLOTS = 32
D_WIN = 2048
FT = 3584
FF_ALL = 28672
N_TENSOR = 8


def draw_scales(key, count):
    base = jnp.exp(jax.random.uniform(key, (count,), jnp.float32, math.log(0.3), math.log(3.0)))
    ramp = jnp.exp(math.log(3.0) * jnp.arange(count, dtype=jnp.float32) / count)
    return base * ramp


def mixed_factors(key_left, key_right, spread):
    left_factor = jax.random.randint(key_left, (D_WIN, BS), -spread, spread + 1).astype(jnp.float32)
    right_factor = jax.random.randint(key_right, (BS, FF_ALL), -spread, spread + 1).astype(jnp.float32)
    return jnp.dot(left_factor, right_factor, precision=lax.Precision.HIGHEST) / 32.0


def draw_gradient(key, part):
    key = jax.random.fold_in(key, 11)
    key_rows, key_cols, key_left, key_right = jax.random.split(key, 4)
    row_scale = draw_scales(key_rows, D_WIN)
    col_scale = draw_scales(key_cols, FF_ALL)
    values = mixed_factors(key_left, key_right, 3)
    return (values * row_scale[:, None] * col_scale[None, :]).astype(jnp.bfloat16)


def draw_definite(key, spread, ridge_term):
    identity = jnp.eye(BS, dtype=jnp.float32)

    def one_slice(slice_key):
        factors = jax.random.randint(slice_key, (SLOTS, BS, BS), -spread, spread + 1).astype(jnp.float32)
        product = jnp.einsum('sik,sjk->sij', factors, factors, precision=lax.Precision.HIGHEST)
        return product / (2.0 * BS) + ridge_term * identity
    return lax.map(one_slice, jax.random.split(key, N_TENSOR))


def draw_prev_left(key, part):
    key = jax.random.fold_in(key, 12)
    return draw_definite(key, 3, 0.05)


def draw_prev_right(key, part):
    key = jax.random.fold_in(key, 13)
    return draw_definite(key, 3, 0.05)


def owner_slice(slice_key):
    key_own, key_rows = jax.random.split(slice_key)
    chosen = jax.random.permutation(key_own, SLOTS // CAP)
    row_keys = jax.random.split(key_rows, CBT)
    orders = jax.vmap(lambda row_key: jax.random.permutation(row_key, NRB))(row_keys)
    position = jnp.argsort(orders, axis=1)
    numbers = jnp.arange(CBT, dtype=jnp.int32)[:, None] * NRB + position.astype(jnp.int32)
    return chosen[numbers // CAP].T


def draw_owner(key, part):
    key = jax.random.fold_in(key, 14)
    slice_keys = jax.random.split(key, N_TENSOR)
    return jax.vmap(owner_slice)(slice_keys).astype(jnp.int32)


def setup_inputs(seed: int = 0) -> dict:
    streams_of = jax.random.split(jax.random.key(seed), 5)
    return {
        "gradient": draw_gradient(jax.random.fold_in(streams_of[4], 71), 0),
        "owner": draw_owner(jax.random.fold_in(streams_of[4], 71), 0),
        "prev_left": draw_prev_left(jax.random.fold_in(streams_of[4], 71), 0),
        "prev_right": draw_prev_right(jax.random.fold_in(streams_of[4], 71), 0),
    }


DECAY = 0.9
EPSILON = 1e-06

def matmul_full(left, right):
    return jnp.dot(left, right, precision=lax.Precision.HIGHEST, preferred_element_type=jnp.float32)

def inverse_root(stats):
    identity = jnp.eye(stats.shape[0], dtype=jnp.float32)
    frob_norm = jnp.sqrt(jnp.sum(stats * stats) + EPSILON)
    normed = stats / frob_norm
    step_one = (5.0 * identity - normed) * 0.25
    square = matmul_full(step_one, step_one)
    fourth = matmul_full(square, square)
    updated = matmul_full(fourth, normed)
    step_two = (5.0 * identity - updated) * 0.25
    return matmul_full(step_one, step_two) * frob_norm ** (-0.25)

def left_gram(block):
    return jnp.dot(block, block.T, preferred_element_type=jnp.float32)

def right_gram(block):
    return jnp.dot(block.T, block, preferred_element_type=jnp.float32)

def reference(gradient, owner, prev_left, prev_right):
    count = NRB * CBT
    positions = jnp.arange(count, dtype=jnp.int32)
    earlier = positions[None, :] < positions[:, None]
    new_left = []
    new_right = []
    results = []
    for tensor_id in range(N_TENSOR):
        slab = gradient[:, tensor_id * FT:(tensor_id + 1) * FT]
        blocks = slab.reshape(NRB, BS, CBT, BS).transpose(0, 2, 1, 3).reshape(count, BS, BS)
        owner_flat = owner[tensor_id].reshape(count).astype(jnp.int32)
        same_owner = owner_flat[None, :] == owner_flat[:, None]
        order_rank = lax.optimization_barrier(jnp.sum((same_owner & earlier).astype(jnp.int32), axis=1)).astype(jnp.int32)
        slot_of = (owner_flat * CAP + order_rank).astype(jnp.int32)
        gram_left = lax.map(left_gram, blocks) / BS
        gram_right = lax.map(right_gram, blocks) / BS
        zeros_left = jnp.zeros(prev_left[tensor_id].shape, jnp.float32).at[slot_of].add(gram_left)
        zeros_right = jnp.zeros(prev_right[tensor_id].shape, jnp.float32).at[slot_of].add(gram_right)
        stats_left = DECAY * prev_left[tensor_id] + (1.0 - DECAY) * zeros_left
        stats_right = DECAY * prev_right[tensor_id] + (1.0 - DECAY) * zeros_right

        def precondition(index, stats_left=stats_left, stats_right=stats_right, blocks=blocks, slot_of=slot_of):
            block = blocks[index]
            root_left = inverse_root(stats_left[slot_of[index]]).astype(jnp.bfloat16)
            root_right = inverse_root(stats_right[slot_of[index]]).astype(jnp.bfloat16)
            half_done = jnp.dot(block, root_right, preferred_element_type=jnp.float32).astype(jnp.bfloat16)
            return jnp.dot(root_left, half_done, preferred_element_type=jnp.float32)
        results.append(lax.map(precondition, positions))
        new_left.append(stats_left)
        new_right.append(stats_right)
    grad_sq = jnp.sum(jnp.square(gradient.astype(jnp.float32)))
    cond_sq = jnp.sum(jnp.stack([jnp.sum(result * result) for result in results]))
    graft_scale = jnp.sqrt(grad_sq / (cond_sq + EPSILON))
    slabs = []
    for result in results:
        packed = lax.optimization_barrier(result.astype(jnp.bfloat16))
        scaled = (graft_scale * packed.astype(jnp.float32)).astype(jnp.bfloat16)
        slabs.append(scaled.reshape(NRB, CBT, BS, BS).transpose(0, 2, 1, 3).reshape(D_WIN, FT))
    return (jnp.concatenate(slabs, axis=1), jnp.stack(new_left), jnp.stack(new_right))
```

```python
import functools

import jax
import jax.numpy as jnp
from jax import lax
from jax.experimental import pallas as pl
from jax.experimental.pallas import tpu as pltpu
from jax.sharding import Mesh
from jax.sharding import PartitionSpec as P

DECAY = 0.9
EPSILON = 1e-06
NX = 4
NZ = 8
NT = 8
COLS = 7
BS = 512
VMEM_LIMIT = 48 * 1024 * 1024

T5 = [3.0517578125, -3.0517578125, 1.220703125, -0.244140625, 0.0244140625, -0.0009765625]
C0 = 25.0 / 16.0
C1 = -5.0 / 16.0 - T5[0] / 4.0
C2, C3, C4, C5, C6 = (-t / 4.0 for t in T5[1:])


def slot_of(owner):
    return (owner & (NZ - 1)) * NX + (owner >> 3)


def scatter_kernel(owner_ref, rows_ref, out_ref):
    out_ref[...] = jnp.zeros_like(out_ref)
    for i in range(NX):
        for j in range(COLS):
            out_ref[slot_of(owner_ref[i, j])] = rows_ref[i, :, j * BS : (j + 1) * BS]


def gather_kernel(owner_ref, scale_ref, slots_ref, out_ref):
    scale = scale_ref[0, 0]
    for i in range(NX):
        for j in range(COLS):
            piece = slots_ref[slot_of(owner_ref[i, j])].astype(jnp.float32)
            out_ref[i, :, j * BS : (j + 1) * BS] = (scale * piece).astype(jnp.bfloat16)


def dot(a, b):
    return jnp.dot(a, b, preferred_element_type=jnp.float32)


def dot_nt(a, b):
    return lax.dot_general(a, b, (((1,), (1,)), ((), ())), preferred_element_type=jnp.float32)


def dot_tn(a, b):
    return lax.dot_general(a, b, (((0,), (0,)), ((), ())), preferred_element_type=jnp.float32)


def split(x):
    high = x.astype(jnp.bfloat16)
    return high, (x - high.astype(jnp.float32)).astype(jnp.bfloat16)


def dot3(a, b):
    return dot(a[0], b[0]) + (dot(a[0], b[1]) + dot(a[1], b[0]))


def root(stats):
    frob = jnp.sqrt(jnp.sum(stats * stats, keepdims=True) + EPSILON)
    n = stats * (1.0 / frob)
    n_parts = split(n)
    x = dot3(n_parts, n_parts)
    x_parts = split(x)
    tail = C4 * x + dot(x_parts[0], (C5 * n + C6 * x).astype(jnp.bfloat16))
    y = dot3(x_parts, split(C3 * n + tail))
    row = lax.broadcasted_iota(jnp.int32, n.shape, 0)
    col = lax.broadcasted_iota(jnp.int32, n.shape, 1)
    total = jnp.where(row == col, C0, 0.0) + (C1 * n + C2 * x) + y
    return (total * lax.rsqrt(jnp.sqrt(frob))).astype(jnp.bfloat16)


def refresh_kernel(block_ref, left_ref, right_ref, packed_ref, left_out, right_out, sum_ref):
    block = block_ref[...]
    right = DECAY * right_ref[...] + ((1.0 - DECAY) / BS) * dot_tn(block, block)
    right_out[...] = right
    left = DECAY * left_ref[...] + ((1.0 - DECAY) / BS) * dot_nt(block, block)
    left_out[...] = left
    half = dot(block, root(right)).astype(jnp.bfloat16)
    conditioned = dot(root(left), half)
    packed_ref[...] = conditioned.astype(jnp.bfloat16)
    sum_ref[...] = jnp.broadcast_to(
        jnp.sum(conditioned * conditioned, keepdims=True), sum_ref.shape
    )


SMEM = functools.partial(pl.BlockSpec, memory_space=pltpu.SMEM)
VMEM = functools.partial(pl.BlockSpec, memory_space=pltpu.VMEM)
PARAMS = pltpu.CompilerParams(vmem_limit_bytes=VMEM_LIMIT)


def body(gradient, owner, prev_left, prev_right):
    rows, cols = gradient.shape
    part = rows // NX
    table = owner[0]
    f32, bf16 = jnp.float32, jnp.bfloat16

    spread = lax.all_to_all(gradient.reshape(NX, part, cols), "x", 0, 0, tiled=True)
    slots = pl.pallas_call(
        scatter_kernel,
        out_shape=jax.ShapeDtypeStruct((NX * NZ, part, BS), bf16),
        in_specs=[SMEM(), VMEM()],
        out_specs=VMEM(),
        compiler_params=PARAMS,
        name="scatter",
    )(table, spread)
    block = lax.all_to_all(slots, ("z", "x"), 0, 0, tiled=True).reshape(BS, BS)
    grad_local = jnp.sum(jnp.square(gradient.astype(f32)))

    packed, left, right, cond = pl.pallas_call(
        refresh_kernel,
        out_shape=[
            jax.ShapeDtypeStruct((BS, BS), bf16),
            jax.ShapeDtypeStruct((BS, BS), f32),
            jax.ShapeDtypeStruct((BS, BS), f32),
            jax.ShapeDtypeStruct((8, 128), f32),
        ],
        in_specs=[VMEM()] * 3,
        out_specs=[VMEM()] * 4,
        compiler_params=PARAMS,
        name="refresh",
    )(block, prev_left[0, 0], prev_right[0, 0])

    returned = lax.all_to_all(packed.reshape(NX * NZ, part, BS), ("z", "x"), 0, 0, tiled=True)
    both = jnp.stack([jnp.full((8, 128), grad_local, f32), cond])
    both = jnp.sum(
        lax.all_to_all(jnp.broadcast_to(both, (NX * NZ, 2, 8, 128)), ("z", "x"), 0, 0, tiled=True), 0
    )
    both = jnp.sum(
        lax.all_to_all(jnp.broadcast_to(both, (NT, 2, 8, 128)), ("y", "c"), 0, 0, tiled=True), 0
    )
    scale = jnp.sqrt(both[0, :1, :1] / (both[1, :1, :1] + EPSILON))
    update = pl.pallas_call(
        gather_kernel,
        out_shape=jax.ShapeDtypeStruct((NX, part, cols), bf16),
        in_specs=[SMEM(), SMEM(), VMEM()],
        out_specs=VMEM(),
        compiler_params=PARAMS,
        name="gather",
    )(table, scale, returned)
    update = lax.all_to_all(update, "x", 0, 0, tiled=True).reshape(rows, cols)
    return update, left[None, None], right[None, None]


def solution(mesh):
    wide = Mesh(mesh.devices.reshape(NX, NZ, NT // 2, 2), ("x", "z", "y", "c"))
    dp, tensor = ("x", "z"), ("y", "c")
    return jax.shard_map(
        body,
        mesh=wide,
        in_specs=(
            P(dp, tensor),
            P(tensor, None, None),
            P(tensor, dp, None, None),
            P(tensor, dp, None, None),
        ),
        out_specs=(P(dp, tensor), P(tensor, dp, None, None), P(tensor, dp, None, None)),
        check_vma=False,
    )
```

```python
import functools

import jax
import jax.numpy as jnp
from jax import lax
from jax.experimental import pallas as pl
from jax.experimental.pallas import tpu as pltpu
from jax.sharding import Mesh
from jax.sharding import PartitionSpec as P

DECAY = 0.9
EPSILON = 1e-06
NX = 4
NZ = 8
NT = 8
COLS = 7
BS = 512
LANES = 128
TILES = BS // LANES
PART = 16
EXTRA = 8
VMEM_LIMIT = 48 * 1024 * 1024

T5 = [3.0517578125, -3.0517578125, 1.220703125, -0.244140625, 0.0244140625, -0.0009765625]
C0 = 25.0 / 16.0
C1 = -5.0 / 16.0 - T5[0] / 4.0
C2, C3, C4, C5, C6 = (-t / 4.0 for t in T5[1:])


def slot_of(owner):
    return (owner & (NZ - 1)) * NX + (owner >> 3)


def scatter_kernel(owner_ref, rows_ref, out_ref):
    out_ref[...] = jnp.zeros_like(out_ref)
    for i in range(NX):
        for j in range(COLS):
            out_ref[slot_of(owner_ref[i, j])] = rows_ref[i, :, j * BS : (j + 1) * BS]


def gather_kernel(owner_ref, slots_ref, out_ref, sums_ref):
    for i in range(NX):
        for j in range(COLS):
            slot = slot_of(owner_ref[i, j])
            for t in range(TILES):
                out_ref[i, :, j * BS + t * LANES : j * BS + (t + 1) * LANES] = slots_ref[
                    slot, t * PART : (t + 1) * PART, :
                ]
    lines = jnp.sum(slots_ref[:, TILES * PART :, :].astype(jnp.float32), axis=0)
    grad = lines[0:1] + (lines[1:2] + lines[2:3])
    cond = lines[3:4] + (lines[4:5] + lines[5:6])
    line = lax.broadcasted_iota(jnp.int32, sums_ref.shape, 0)
    sums_ref[...] = jnp.where(line < 4, grad, cond)


def finish_kernel(sums_ref, rows_ref, out_ref):
    scale = jnp.sqrt(sums_ref[0:1, 0:1] / (sums_ref[4:5, 0:1] + EPSILON))
    out_ref[...] = (scale * rows_ref[...].astype(jnp.float32)).astype(jnp.bfloat16)


def dot(a, b):
    return jnp.dot(a, b, preferred_element_type=jnp.float32)


def dot_nt(a, b):
    return lax.dot_general(a, b, (((1,), (1,)), ((), ())), preferred_element_type=jnp.float32)


def dot_tn(a, b):
    return lax.dot_general(a, b, (((0,), (0,)), ((), ())), preferred_element_type=jnp.float32)


def split(x):
    high = x.astype(jnp.bfloat16)
    return high, (x - high.astype(jnp.float32)).astype(jnp.bfloat16)


def dot3(a, b):
    return dot(a[0], b[0]) + (dot(a[0], b[1]) + dot(a[1], b[0]))


def root(stats):
    frob = jnp.sqrt(jnp.sum(stats * stats, keepdims=True) + EPSILON)
    n = stats * (1.0 / frob)
    n_parts = split(n)
    x = dot3(n_parts, n_parts)
    x_parts = split(x)
    tail = C4 * x + dot(x_parts[0], (C5 * n + C6 * x).astype(jnp.bfloat16))
    y = dot3(x_parts, split(C3 * n + tail))
    row = lax.broadcasted_iota(jnp.int32, n.shape, 0)
    col = lax.broadcasted_iota(jnp.int32, n.shape, 1)
    total = jnp.where(row == col, C0, 0.0) + (C1 * n + C2 * x) + y
    return (total * lax.rsqrt(jnp.sqrt(frob))).astype(jnp.bfloat16)


def refresh_kernel(
    grad_ref, block_ref, left_ref, right_ref, packed_ref, left_out, right_out
):
    block = block_ref[...]
    right = DECAY * right_ref[...] + ((1.0 - DECAY) / BS) * dot_tn(block, block)
    right_out[...] = right
    left = DECAY * left_ref[...] + ((1.0 - DECAY) / BS) * dot_nt(block, block)
    left_out[...] = left
    half = dot(block, root(right)).astype(jnp.bfloat16)
    conditioned = dot(root(left), half)
    packed = conditioned.astype(jnp.bfloat16)
    for t in range(TILES):
        packed_ref[:, t * PART : (t + 1) * PART, :] = packed[
            :, t * LANES : (t + 1) * LANES
        ].reshape(NX * NZ, PART, LANES)
    line = lax.broadcasted_iota(jnp.int32, (EXTRA, LANES), 0)
    rest = jnp.where(line < 3, grad_ref[0, 0], jnp.sum(conditioned * conditioned, keepdims=True))
    high = rest.astype(jnp.bfloat16).astype(jnp.float32)
    rest = rest - high
    middle = rest.astype(jnp.bfloat16).astype(jnp.float32)
    low = rest - middle
    kind = jnp.where(line < 3, line, line - 3)
    terms = jnp.where(kind == 0, high, jnp.where(kind == 1, middle, low)).astype(jnp.bfloat16)
    packed_ref[:, TILES * PART :, :] = jnp.broadcast_to(terms[None], (NX * NZ, EXTRA, LANES))


SMEM = functools.partial(pl.BlockSpec, memory_space=pltpu.SMEM)
VMEM = functools.partial(pl.BlockSpec, memory_space=pltpu.VMEM)
PARAMS = pltpu.CompilerParams(vmem_limit_bytes=VMEM_LIMIT)


def total(value):
    for axis, partner in (("c", (1, 0)), ("y", (1, 0, 3, 2)), ("y", (3, 2, 1, 0))):
        value = value + lax.ppermute(value, axis, list(enumerate(partner)))
    return value


def body(gradient, owner, prev_left, prev_right):
    rows, cols = gradient.shape
    part = rows // NX
    table = owner[0]
    f32, bf16 = jnp.float32, jnp.bfloat16

    spread = lax.all_to_all(gradient.reshape(NX, part, cols), "x", 0, 0, tiled=True)
    slots = pl.pallas_call(
        scatter_kernel,
        out_shape=jax.ShapeDtypeStruct((NX * NZ, part, BS), bf16),
        in_specs=[SMEM(), VMEM()],
        out_specs=VMEM(),
        compiler_params=PARAMS,
        name="scatter",
    )(table, spread)
    block = lax.all_to_all(slots, ("z", "x"), 0, 0, tiled=True).reshape(BS, BS)
    grad_local = jnp.sum(jnp.square(gradient.astype(f32)))

    packed, left, right = pl.pallas_call(
        refresh_kernel,
        out_shape=[
            jax.ShapeDtypeStruct((NX * NZ, TILES * PART + EXTRA, LANES), bf16),
            jax.ShapeDtypeStruct((BS, BS), f32),
            jax.ShapeDtypeStruct((BS, BS), f32),
        ],
        in_specs=[SMEM()] + [VMEM()] * 3,
        out_specs=[VMEM()] * 3,
        compiler_params=PARAMS,
        name="refresh",
    )(grad_local.reshape(1, 1), block, prev_left[0, 0], prev_right[0, 0])

    returned = lax.all_to_all(packed, ("z", "x"), 0, 0, tiled=True)
    update, sums = pl.pallas_call(
        gather_kernel,
        out_shape=[
            jax.ShapeDtypeStruct((NX, part, cols), bf16),
            jax.ShapeDtypeStruct((8, LANES), f32),
        ],
        in_specs=[SMEM(), VMEM()],
        out_specs=[VMEM()] * 2,
        compiler_params=PARAMS,
        name="gather",
    )(table, returned)
    update = lax.all_to_all(update, "x", 0, 0, tiled=True).reshape(rows, cols)
    update = pl.pallas_call(
        finish_kernel,
        out_shape=jax.ShapeDtypeStruct((rows, cols), bf16),
        in_specs=[VMEM()] * 2,
        out_specs=VMEM(),
        compiler_params=PARAMS,
        name="finish",
    )(total(sums), update)
    return update, left[None, None], right[None, None]


def solution(mesh):
    wide = Mesh(mesh.devices.reshape(NX, NZ, NT // 2, 2), ("x", "z", "y", "c"))
    dp, tensor = ("x", "z"), ("y", "c")
    return jax.shard_map(
        body,
        mesh=wide,
        in_specs=(
            P(dp, tensor),
            P(tensor, None, None),
            P(tensor, dp, None, None),
            P(tensor, dp, None, None),
        ),
        out_specs=(P(dp, tensor), P(tensor, dp, None, None), P(tensor, dp, None, None)),
        check_vma=False,
    )
```

```python
import functools

import jax
import jax.numpy as jnp
from jax import lax
from jax.experimental import pallas as pl
from jax.experimental.pallas import tpu as pltpu
from jax.sharding import Mesh
from jax.sharding import PartitionSpec as P

DECAY = 0.9
EPSILON = 1e-06
NX = 4
NZ = 8
NT = 8
COLS = 7
BS = 512
LANES = 128
TILES = BS // LANES
PART = 16
EXTRA = 8
VMEM_LIMIT = 48 * 1024 * 1024

T5 = [3.0517578125, -3.0517578125, 1.220703125, -0.244140625, 0.0244140625, -0.0009765625]
C0 = 25.0 / 16.0
C1 = -5.0 / 16.0 - T5[0] / 4.0
C2, C3, C4, C5, C6 = (-t / 4.0 for t in T5[1:])


def scatter_kernel(owner_ref, rows_ref, out_ref):
    out_ref[...] = jnp.zeros_like(out_ref)
    for i in range(NX):
        for j in range(COLS):
            out_ref[owner_ref[i, j]] = rows_ref[i, :, j * BS : (j + 1) * BS]


def sums_kernel(slots_ref, sums_ref):
    lines = jnp.sum(slots_ref[:, TILES * PART :, :].astype(jnp.float32), axis=0)
    grad = lines[0:1] + (lines[1:2] + lines[2:3])
    cond = lines[3:4] + (lines[4:5] + lines[5:6])
    line = lax.broadcasted_iota(jnp.int32, sums_ref.shape, 0)
    sums_ref[...] = jnp.where(line < 4, grad, cond)


def gather_kernel(owner_ref, after_ref, slots_ref, *out_refs):
    del after_ref
    for k, out_ref in enumerate(out_refs):
        for j in range(COLS):
            slot = owner_ref[NX + k, j]
            for t in range(TILES):
                out_ref[:, j * BS + t * LANES : j * BS + (t + 1) * LANES] = slots_ref[
                    slot, t * PART : (t + 1) * PART, :
                ]


def finish_kernel(x_ref, sums_ref, *refs):
    scale = jnp.sqrt(sums_ref[0:1, 0:1] / (sums_ref[4:5, 0:1] + EPSILON))
    out_ref = refs[NX]
    for k in range(NX):
        start = pl.multiple_of(((x_ref[0, 0] + NX - k) & (NX - 1)) * PART, PART)
        out_ref[pl.ds(start, PART), :] = (scale * refs[k][...].astype(jnp.float32)).astype(
            jnp.bfloat16
        )


def dot(a, b):
    return jnp.dot(a, b, preferred_element_type=jnp.float32)


def dot_nt(a, b):
    return lax.dot_general(a, b, (((1,), (1,)), ((), ())), preferred_element_type=jnp.float32)


def dot_tn(a, b):
    return lax.dot_general(a, b, (((0,), (0,)), ((), ())), preferred_element_type=jnp.float32)


def split(x):
    high = x.astype(jnp.bfloat16)
    return high, (x - high.astype(jnp.float32)).astype(jnp.bfloat16)


def normalize(stats):
    frob = jnp.sqrt(jnp.sum(stats * stats, keepdims=True) + EPSILON)
    return frob, stats * (1.0 / frob)


def square(n):
    high = n.astype(jnp.bfloat16)
    low2 = (2.0 * (n - high.astype(jnp.float32))).astype(jnp.bfloat16)
    return high, dot(high, high) + dot(high, low2)


def upper_terms(n, n_high, x):
    x_high = x.astype(jnp.bfloat16)
    mixed = n_high * jnp.bfloat16(C5) + x_high * jnp.bfloat16(C6)
    high, low = split(C3 * n + (C4 * x + dot(x_high, mixed)))
    return dot(x_high, high) + dot(x_high, low)


def write_root(root_ref, frob, n, x, upper):
    scale = lax.rsqrt(jnp.sqrt(frob))
    total = (C1 * n + C2 * x) + upper
    root_ref[...] = (total * scale).astype(jnp.bfloat16)
    row = lax.broadcasted_iota(jnp.int32, (LANES, LANES), 0)
    col = lax.broadcasted_iota(jnp.int32, (LANES, LANES), 1)
    constant = jnp.where(row == col, C0, 0.0)
    for t in range(TILES):
        span = slice(t * LANES, (t + 1) * LANES)
        root_ref[span, span] = ((total[span, span] + constant) * scale).astype(jnp.bfloat16)


def refresh_kernel(
    block_ref, left_ref, right_ref, packed_ref, left_out, right_out,
    ordered, left_root, right_root
):
    for p in range(NX):
        for z in range(NZ):
            row = (z * NX + p) * PART
            ordered[row : row + PART, :] = block_ref[p * NZ + z]
    block = ordered[...]
    right = DECAY * right_ref[...] + ((1.0 - DECAY) / BS) * dot_tn(block, block)
    right_out[...] = right
    left = DECAY * left_ref[...] + ((1.0 - DECAY) / BS) * dot_nt(block, block)
    left_out[...] = left
    wide = block.astype(jnp.float32)
    grad_sq = jnp.sum(wide * wide, keepdims=True)
    right_frob, right_n = normalize(right)
    left_frob, left_n = normalize(left)
    right_high, right_x = square(right_n)
    left_high, left_x = square(left_n)
    right_upper = upper_terms(right_n, right_high, right_x)
    left_upper = upper_terms(left_n, left_high, left_x)
    write_root(right_root, right_frob, right_n, right_x, right_upper)
    half = dot(block, right_root[...]).astype(jnp.bfloat16)
    write_root(left_root, left_frob, left_n, left_x, left_upper)
    conditioned = dot(left_root[...], half)
    packed = conditioned.astype(jnp.bfloat16)
    for t in range(TILES):
        tile = packed[:, t * LANES : (t + 1) * LANES].reshape(NZ, NX, PART, LANES)
        for p in range(NX):
            packed_ref[p * NZ : (p + 1) * NZ, t * PART : (t + 1) * PART, :] = tile[:, p]
    line = lax.broadcasted_iota(jnp.int32, (EXTRA, LANES), 0)
    rest = jnp.where(line < 3, grad_sq, jnp.sum(conditioned * conditioned, keepdims=True))
    high = rest.astype(jnp.bfloat16).astype(jnp.float32)
    rest = rest - high
    middle = rest.astype(jnp.bfloat16).astype(jnp.float32)
    low = rest - middle
    kind = jnp.where(line < 3, line, line - 3)
    terms = jnp.where(kind == 0, high, jnp.where(kind == 1, middle, low)).astype(jnp.bfloat16)
    packed_ref[:, TILES * PART :, :] = jnp.broadcast_to(terms[None], (NX * NZ, EXTRA, LANES))


SMEM = functools.partial(pl.BlockSpec, memory_space=pltpu.SMEM)
VMEM = functools.partial(pl.BlockSpec, memory_space=pltpu.VMEM)
PARAMS = pltpu.CompilerParams(vmem_limit_bytes=VMEM_LIMIT)


def add_other(value, axis, partner):
    return value + lax.ppermute(value, axis, list(enumerate(partner)))


def body(gradient, owner, prev_left, prev_right):
    rows, cols = gradient.shape
    part = rows // NX
    place = lax.axis_index("x")
    table = jnp.clip(owner[0], 0, NX * NZ - 1)
    table = jnp.concatenate([table, jnp.roll(table, -place, axis=0)])
    f32, bf16 = jnp.float32, jnp.bfloat16

    spread = lax.all_to_all(gradient.reshape(NX, part, cols), "x", 0, 0, tiled=True)
    slots = pl.pallas_call(
        scatter_kernel,
        out_shape=jax.ShapeDtypeStruct((NX * NZ, part, BS), bf16),
        in_specs=[SMEM(), VMEM()],
        out_specs=VMEM(),
        compiler_params=PARAMS,
        name="scatter",
    )(table, spread)
    block = lax.all_to_all(slots, ("x", "z"), 0, 0, tiled=True)

    packed, left, right = pl.pallas_call(
        refresh_kernel,
        out_shape=[
            jax.ShapeDtypeStruct((NX * NZ, TILES * PART + EXTRA, LANES), bf16),
            jax.ShapeDtypeStruct((BS, BS), f32),
            jax.ShapeDtypeStruct((BS, BS), f32),
        ],
        in_specs=[VMEM()] * 3,
        out_specs=[VMEM()] * 3,
        scratch_shapes=[pltpu.VMEM((BS, BS), bf16)] * 3,
        compiler_params=PARAMS,
        name="refresh",
    )(block, prev_left[0, 0], prev_right[0, 0])

    returned = lax.all_to_all(packed, ("x", "z"), 0, 0, tiled=True)
    sums = pl.pallas_call(
        sums_kernel,
        out_shape=jax.ShapeDtypeStruct((8, LANES), f32),
        in_specs=[VMEM()],
        out_specs=VMEM(),
        compiler_params=PARAMS,
        name="sums",
    )(returned)
    sums = add_other(sums, "c", (1, 0))
    pieces = pl.pallas_call(
        gather_kernel,
        out_shape=[jax.ShapeDtypeStruct((part, cols), bf16)] * NX,
        in_specs=[SMEM(), pl.BlockSpec(memory_space=pl.ANY), VMEM()],
        out_specs=[VMEM()] * NX,
        compiler_params=PARAMS,
        name="gather",
    )(table, sums, returned)
    sums = add_other(add_other(sums, "y", (1, 0, 3, 2)), "y", (3, 2, 1, 0))
    moved = [pieces[0]] + [
        lax.ppermute(pieces[k], "x", [(i, (i + k) % NX) for i in range(NX)]) for k in range(1, NX)
    ]
    update = pl.pallas_call(
        finish_kernel,
        out_shape=jax.ShapeDtypeStruct((rows, cols), bf16),
        in_specs=[SMEM()] + [VMEM()] * (NX + 1),
        out_specs=VMEM(),
        compiler_params=PARAMS,
        name="finish",
    )(place.reshape(1, 1), sums, *moved)
    return update, left[None, None], right[None, None]


def solution(mesh):
    wide = Mesh(mesh.devices.reshape(NX, NZ, NT // 2, 2), ("x", "z", "y", "c"))
    dp, tensor = ("x", "z"), ("y", "c")
    return jax.shard_map(
        body,
        mesh=wide,
        in_specs=(
            P(dp, tensor),
            P(tensor, None, None),
            P(tensor, dp, None, None),
            P(tensor, dp, None, None),
        ),
        out_specs=(P(dp, tensor), P(tensor, dp, None, None), P(tensor, dp, None, None)),
        check_vma=False,
    )
```

```python
import functools

import jax
import jax.numpy as jnp
from jax import lax
from jax.experimental import pallas as pl
from jax.experimental.pallas import tpu as pltpu
from jax.sharding import Mesh
from jax.sharding import PartitionSpec as P

DECAY = 0.9
EPSILON = 1e-06
NX = 4
NZ = 8
NT = 8
COLS = 7
BS = 512
LANES = 128
TILES = BS // LANES
PART = 16
EXTRA = 8
VMEM_LIMIT = 48 * 1024 * 1024

T5 = [3.0517578125, -3.0517578125, 1.220703125, -0.244140625, 0.0244140625, -0.0009765625]
C0 = 25.0 / 16.0
C1 = -5.0 / 16.0 - T5[0] / 4.0
C2, C3, C4, C5, C6 = (-t / 4.0 for t in T5[1:])


def scatter_kernel(owner_ref, rows_ref, out_ref):
    out_ref[...] = jnp.zeros_like(out_ref)
    for i in range(NX):
        for j in range(COLS):
            out_ref[owner_ref[i, j]] = rows_ref[i, :, j * BS : (j + 1) * BS]


def sums_kernel(slots_ref, sums_ref):
    lines = jnp.sum(slots_ref[:, TILES * PART :, :].astype(jnp.float32), axis=0)
    grad = lines[0:1] + (lines[1:2] + lines[2:3])
    cond = lines[3:4] + (lines[4:5] + lines[5:6])
    line = lax.broadcasted_iota(jnp.int32, sums_ref.shape, 0)
    sums_ref[...] = jnp.where(line < 4, grad, cond)


def gather_kernel(turns, owner_ref, after_ref, slots_ref, *out_refs):
    del after_ref
    for k, out_ref in zip(turns, out_refs):
        for j in range(COLS):
            slot = owner_ref[NX + k, j]
            for t in range(TILES):
                out_ref[:, j * BS + t * LANES : j * BS + (t + 1) * LANES] = slots_ref[
                    slot, t * PART : (t + 1) * PART, :
                ]


def finish_kernel(x_ref, sums_ref, *refs):
    scale = jnp.sqrt(sums_ref[0:1, 0:1] / (sums_ref[4:5, 0:1] + EPSILON))
    out_ref = refs[NX]
    for k in range(NX):
        start = pl.multiple_of(((x_ref[0, 0] + NX - k) & (NX - 1)) * PART, PART)
        out_ref[pl.ds(start, PART), :] = (scale * refs[k][...].astype(jnp.float32)).astype(
            jnp.bfloat16
        )


def dot(a, b):
    return jnp.dot(a, b, preferred_element_type=jnp.float32)


def dot_nt(a, b):
    return lax.dot_general(a, b, (((1,), (1,)), ((), ())), preferred_element_type=jnp.float32)


def dot_tn(a, b):
    return lax.dot_general(a, b, (((0,), (0,)), ((), ())), preferred_element_type=jnp.float32)


def split(x):
    high = x.astype(jnp.bfloat16)
    return high, (x - high.astype(jnp.float32)).astype(jnp.bfloat16)


def normalize(stats):
    frob = jnp.sqrt(jnp.sum(stats * stats, keepdims=True) + EPSILON)
    return frob, stats * (1.0 / frob)


def square(n):
    high = n.astype(jnp.bfloat16)
    low2 = (2.0 * (n - high.astype(jnp.float32))).astype(jnp.bfloat16)
    return high, dot(high, high) + dot(high, low2)


def upper_terms(n, n_high, x):
    x_high = x.astype(jnp.bfloat16)
    mixed = n_high * jnp.bfloat16(C5) + x_high * jnp.bfloat16(C6)
    high, low = split(C3 * n + (C4 * x + dot(x_high, mixed)))
    return dot(x_high, high) + dot(x_high, low)


def write_root(root_ref, frob, n, x, upper):
    scale = lax.rsqrt(jnp.sqrt(frob))
    total = (C1 * n + C2 * x) + upper
    root_ref[...] = (total * scale).astype(jnp.bfloat16)
    row = lax.broadcasted_iota(jnp.int32, (LANES, LANES), 0)
    col = lax.broadcasted_iota(jnp.int32, (LANES, LANES), 1)
    constant = jnp.where(row == col, C0, 0.0)
    for t in range(TILES):
        span = slice(t * LANES, (t + 1) * LANES)
        root_ref[span, span] = ((total[span, span] + constant) * scale).astype(jnp.bfloat16)


def refresh_kernel(
    block_ref, left_ref, right_ref, packed_ref, left_out, right_out,
    ordered, left_root, right_root
):
    for p in range(NX):
        for z in range(NZ):
            row = (z * NX + p) * PART
            ordered[row : row + PART, :] = block_ref[p * NZ + z]
    block = ordered[...]
    right = DECAY * right_ref[...] + ((1.0 - DECAY) / BS) * dot_tn(block, block)
    right_out[...] = right
    left = DECAY * left_ref[...] + ((1.0 - DECAY) / BS) * dot_nt(block, block)
    left_out[...] = left
    wide = block.astype(jnp.float32)
    grad_sq = jnp.sum(wide * wide, keepdims=True)
    right_frob, right_n = normalize(right)
    left_frob, left_n = normalize(left)
    right_high, right_x = square(right_n)
    left_high, left_x = square(left_n)
    right_upper = upper_terms(right_n, right_high, right_x)
    left_upper = upper_terms(left_n, left_high, left_x)
    write_root(right_root, right_frob, right_n, right_x, right_upper)
    half = dot(block, right_root[...]).astype(jnp.bfloat16)
    write_root(left_root, left_frob, left_n, left_x, left_upper)
    conditioned = dot(left_root[...], half)
    packed = conditioned.astype(jnp.bfloat16)
    for t in range(TILES):
        tile = packed[:, t * LANES : (t + 1) * LANES].reshape(NZ, NX, PART, LANES)
        for p in range(NX):
            packed_ref[p * NZ : (p + 1) * NZ, t * PART : (t + 1) * PART, :] = tile[:, p]
    line = lax.broadcasted_iota(jnp.int32, (EXTRA, LANES), 0)
    rest = jnp.where(line < 3, grad_sq, jnp.sum(conditioned * conditioned, keepdims=True))
    high = rest.astype(jnp.bfloat16).astype(jnp.float32)
    rest = rest - high
    middle = rest.astype(jnp.bfloat16).astype(jnp.float32)
    low = rest - middle
    kind = jnp.where(line < 3, line, line - 3)
    terms = jnp.where(kind == 0, high, jnp.where(kind == 1, middle, low)).astype(jnp.bfloat16)
    packed_ref[:, TILES * PART :, :] = jnp.broadcast_to(terms[None], (NX * NZ, EXTRA, LANES))


SMEM = functools.partial(pl.BlockSpec, memory_space=pltpu.SMEM)
VMEM = functools.partial(pl.BlockSpec, memory_space=pltpu.VMEM)
PARAMS = pltpu.CompilerParams(vmem_limit_bytes=VMEM_LIMIT)


def add_other(value, axis, partner):
    return value + lax.ppermute(value, axis, list(enumerate(partner)))


def body(gradient, owner, prev_left, prev_right):
    rows, cols = gradient.shape
    part = rows // NX
    place = lax.axis_index("x")
    table = jnp.clip(owner[0], 0, NX * NZ - 1)
    table = jnp.concatenate([table, jnp.roll(table, -place, axis=0)])
    f32, bf16 = jnp.float32, jnp.bfloat16

    spread = lax.all_to_all(gradient.reshape(NX, part, cols), "x", 0, 0, tiled=True)
    slots = pl.pallas_call(
        scatter_kernel,
        out_shape=jax.ShapeDtypeStruct((NX * NZ, part, BS), bf16),
        in_specs=[SMEM(), VMEM()],
        out_specs=VMEM(),
        compiler_params=PARAMS,
        name="scatter",
    )(table, spread)
    block = lax.all_to_all(slots, ("x", "z"), 0, 0, tiled=True)

    packed, left, right = pl.pallas_call(
        refresh_kernel,
        out_shape=[
            jax.ShapeDtypeStruct((NX * NZ, TILES * PART + EXTRA, LANES), bf16),
            jax.ShapeDtypeStruct((BS, BS), f32),
            jax.ShapeDtypeStruct((BS, BS), f32),
        ],
        in_specs=[VMEM()] * 3,
        out_specs=[VMEM()] * 3,
        scratch_shapes=[pltpu.VMEM((BS, BS), bf16)] * 3,
        compiler_params=PARAMS,
        name="refresh",
    )(block, prev_left[0, 0], prev_right[0, 0])

    returned = lax.all_to_all(packed, ("x", "z"), 0, 0, tiled=True)
    sums = pl.pallas_call(
        sums_kernel,
        out_shape=jax.ShapeDtypeStruct((8, LANES), f32),
        in_specs=[VMEM()],
        out_specs=VMEM(),
        compiler_params=PARAMS,
        name="sums",
    )(returned)
    sums = add_other(sums, "c", (1, 0))
    def gather(turns, after):
        return pl.pallas_call(
            functools.partial(gather_kernel, turns),
            out_shape=[jax.ShapeDtypeStruct((part, cols), bf16)] * len(turns),
            in_specs=[SMEM(), pl.BlockSpec(memory_space=pl.ANY), VMEM()],
            out_specs=[VMEM()] * len(turns),
            compiler_params=PARAMS,
            name="gather",
        )(table, after, returned)

    def turn(piece, k):
        return lax.ppermute(piece, "x", [(i, (i + k) % NX) for i in range(NX)])

    far, near = gather((2, 1), sums)
    far, near = turn(far, 2), turn(near, 1)
    sums = add_other(sums, "y", (1, 0, 3, 2))
    last, own = gather((3, 0), sums)
    moved = [own, near, far, turn(last, 3)]
    sums = add_other(sums, "y", (3, 2, 1, 0))
    update = pl.pallas_call(
        finish_kernel,
        out_shape=jax.ShapeDtypeStruct((rows, cols), bf16),
        in_specs=[SMEM()] + [VMEM()] * (NX + 1),
        out_specs=VMEM(),
        compiler_params=PARAMS,
        name="finish",
    )(place.reshape(1, 1), sums, *moved)
    return update, left[None, None], right[None, None]


def solution(mesh):
    wide = Mesh(mesh.devices.reshape(NX, NZ, NT // 2, 2), ("x", "z", "y", "c"))
    dp, tensor = ("x", "z"), ("y", "c")
    return jax.shard_map(
        body,
        mesh=wide,
        in_specs=(
            P(dp, tensor),
            P(tensor, None, None),
            P(tensor, dp, None, None),
            P(tensor, dp, None, None),
        ),
        out_specs=(P(dp, tensor), P(tensor, dp, None, None), P(tensor, dp, None, None)),
        check_vma=False,
    )
```

```python
import functools

import jax
import jax.numpy as jnp
from jax import lax
from jax.experimental import pallas as pl
from jax.experimental.pallas import tpu as pltpu
from jax.sharding import Mesh
from jax.sharding import PartitionSpec as P

DECAY = 0.9
EPSILON = 1e-06
NX = 4
NZ = 8
NT = 8
COLS = 7
BS = 512
LANES = 128
TILES = BS // LANES
PART = 16
EXTRA = 8
VMEM_LIMIT = 48 * 1024 * 1024

T5 = [3.0517578125, -3.0517578125, 1.220703125, -0.244140625, 0.0244140625, -0.0009765625]
C0 = 25.0 / 16.0
C1 = -5.0 / 16.0 - T5[0] / 4.0
C2, C3, C4, C5, C6 = (-t / 4.0 for t in T5[1:])


def scatter_kernel(owner_ref, rows_ref, out_ref):
    out_ref[...] = jnp.zeros_like(out_ref)
    for i in range(NX):
        for j in range(COLS):
            out_ref[owner_ref[i, j]] = rows_ref[i, :, j * BS : (j + 1) * BS]


def sums_kernel(slots_ref, sums_ref):
    lines = jnp.sum(slots_ref[:, TILES * PART :, :].astype(jnp.float32), axis=0)
    grad = lines[0:1] + (lines[1:2] + lines[2:3])
    cond = lines[3:4] + (lines[4:5] + lines[5:6])
    line = lax.broadcasted_iota(jnp.int32, sums_ref.shape, 0)
    sums_ref[...] = jnp.where(line < 4, grad, cond)


def gather_kernel(turns, owner_ref, after_ref, slots_ref, *out_refs):
    del after_ref
    for k, out_ref in zip(turns, out_refs):
        for j in range(COLS):
            slot = owner_ref[NX + k, j]
            for t in range(TILES):
                out_ref[:, j * BS + t * LANES : j * BS + (t + 1) * LANES] = slots_ref[
                    slot, t * PART : (t + 1) * PART, :
                ]


def finish_kernel(x_ref, sums_ref, *refs):
    scale = jnp.sqrt(sums_ref[0:1, 0:1] / (sums_ref[4:5, 0:1] + EPSILON))
    out_ref = refs[NX]
    for k in range(NX):
        start = pl.multiple_of(((x_ref[0, 0] + NX - k) & (NX - 1)) * PART, PART)
        out_ref[pl.ds(start, PART), :] = (scale * refs[k][...].astype(jnp.float32)).astype(
            jnp.bfloat16
        )


def dot(a, b):
    return jnp.dot(a, b, preferred_element_type=jnp.float32)


def dot_nt(a, b):
    return lax.dot_general(a, b, (((1,), (1,)), ((), ())), preferred_element_type=jnp.float32)


def dot_tn(a, b):
    return lax.dot_general(a, b, (((0,), (0,)), ((), ())), preferred_element_type=jnp.float32)


def split(x):
    high = x.astype(jnp.bfloat16)
    return high, (x - high.astype(jnp.float32)).astype(jnp.bfloat16)


def normalize(stats):
    frob = jnp.sqrt(jnp.sum(stats * stats, keepdims=True) + EPSILON)
    return frob, stats * (1.0 / frob)


def square(n):
    high = n.astype(jnp.bfloat16)
    low2 = (2.0 * (n - high.astype(jnp.float32))).astype(jnp.bfloat16)
    return high, dot(high, high) + dot(high, low2)


def upper_terms(n, n_high, x):
    x_high = x.astype(jnp.bfloat16)
    mixed = n_high * jnp.bfloat16(C5) + x_high * jnp.bfloat16(C6)
    high, low = split(C3 * n + (C4 * x + dot(x_high, mixed)))
    return dot(x_high, high) + dot(x_high, low)


def write_root(root_ref, frob, n, x, upper):
    scale = lax.rsqrt(jnp.sqrt(frob))
    total = (C1 * n + C2 * x) + upper
    root_ref[...] = (total * scale).astype(jnp.bfloat16)
    row = lax.broadcasted_iota(jnp.int32, (LANES, LANES), 0)
    col = lax.broadcasted_iota(jnp.int32, (LANES, LANES), 1)
    constant = jnp.where(row == col, C0, 0.0)
    for t in range(TILES):
        span = slice(t * LANES, (t + 1) * LANES)
        root_ref[span, span] = ((total[span, span] + constant) * scale).astype(jnp.bfloat16)


def slot_at(x, z):
    return (z & 1) * (NX * NZ // 2) + x * (NZ // 2) + (z >> 1)


def refresh_kernel(
    block_ref, left_ref, right_ref, packed_ref, left_out, right_out,
    ordered, left_root, right_root
):
    for p in range(NX):
        for z in range(NZ):
            row = (z * NX + p) * PART
            ordered[row : row + PART, :] = block_ref[p * NZ + z]
    block = ordered[...]
    right = DECAY * right_ref[...] + ((1.0 - DECAY) / BS) * dot_tn(block, block)
    right_out[...] = right
    left = DECAY * left_ref[...] + ((1.0 - DECAY) / BS) * dot_nt(block, block)
    left_out[...] = left
    wide = block.astype(jnp.float32)
    grad_sq = jnp.sum(wide * wide, keepdims=True)
    right_frob, right_n = normalize(right)
    left_frob, left_n = normalize(left)
    right_high, right_x = square(right_n)
    left_high, left_x = square(left_n)
    right_upper = upper_terms(right_n, right_high, right_x)
    left_upper = upper_terms(left_n, left_high, left_x)
    write_root(right_root, right_frob, right_n, right_x, right_upper)
    half = dot(block, right_root[...]).astype(jnp.bfloat16)
    write_root(left_root, left_frob, left_n, left_x, left_upper)
    conditioned = dot(left_root[...], half)
    packed = conditioned.astype(jnp.bfloat16)
    for t in range(TILES):
        tile = packed[:, t * LANES : (t + 1) * LANES].reshape(NZ, NX, PART, LANES)
        for p in range(NX):
            for z in range(NZ):
                packed_ref[slot_at(p, z), t * PART : (t + 1) * PART, :] = tile[z, p]
    line = lax.broadcasted_iota(jnp.int32, (EXTRA, LANES), 0)
    rest = jnp.where(line < 3, grad_sq, jnp.sum(conditioned * conditioned, keepdims=True))
    high = rest.astype(jnp.bfloat16).astype(jnp.float32)
    rest = rest - high
    middle = rest.astype(jnp.bfloat16).astype(jnp.float32)
    low = rest - middle
    kind = jnp.where(line < 3, line, line - 3)
    terms = jnp.where(kind == 0, high, jnp.where(kind == 1, middle, low)).astype(jnp.bfloat16)
    packed_ref[:, TILES * PART :, :] = jnp.broadcast_to(terms[None], (NX * NZ, EXTRA, LANES))


SMEM = functools.partial(pl.BlockSpec, memory_space=pltpu.SMEM)
VMEM = functools.partial(pl.BlockSpec, memory_space=pltpu.VMEM)
PARAMS = pltpu.CompilerParams(vmem_limit_bytes=VMEM_LIMIT)


def add_other(value, axis, partner):
    return value + lax.ppermute(value, axis, list(enumerate(partner)))


def body(gradient, owner, prev_left, prev_right):
    rows, cols = gradient.shape
    part = rows // NX
    place = lax.axis_index("x")
    table = jnp.clip(owner[0], 0, NX * NZ - 1)
    slot = (table & 1) * (NX * NZ // 2) + (table // NZ) * (NZ // 2) + ((table & (NZ - 1)) >> 1)
    table = jnp.concatenate([table, jnp.roll(slot, -place, axis=0)])
    f32, bf16 = jnp.float32, jnp.bfloat16

    spread = lax.all_to_all(gradient.reshape(NX, part, cols), "x", 0, 0, tiled=True)
    slots = pl.pallas_call(
        scatter_kernel,
        out_shape=jax.ShapeDtypeStruct((NX * NZ, part, BS), bf16),
        in_specs=[SMEM(), VMEM()],
        out_specs=VMEM(),
        compiler_params=PARAMS,
        name="scatter",
    )(table, spread)
    block = lax.all_to_all(slots, ("x", "zh", "zl"), 0, 0, tiled=True)

    packed, left, right = pl.pallas_call(
        refresh_kernel,
        out_shape=[
            jax.ShapeDtypeStruct((NX * NZ, TILES * PART + EXTRA, LANES), bf16),
            jax.ShapeDtypeStruct((BS, BS), f32),
            jax.ShapeDtypeStruct((BS, BS), f32),
        ],
        in_specs=[VMEM()] * 3,
        out_specs=[VMEM()] * 3,
        scratch_shapes=[pltpu.VMEM((BS, BS), bf16)] * 3,
        compiler_params=PARAMS,
        name="refresh",
    )(block, prev_left[0, 0], prev_right[0, 0])

    returned = lax.all_to_all(packed, ("zl", "x", "zh"), 0, 0, tiled=True)
    sums = pl.pallas_call(
        sums_kernel,
        out_shape=jax.ShapeDtypeStruct((8, LANES), f32),
        in_specs=[VMEM()],
        out_specs=VMEM(),
        compiler_params=PARAMS,
        name="sums",
    )(returned)
    sums = add_other(sums, "c", (1, 0))
    def gather(turns, after):
        return pl.pallas_call(
            functools.partial(gather_kernel, turns),
            out_shape=[jax.ShapeDtypeStruct((part, cols), bf16)] * len(turns),
            in_specs=[SMEM(), pl.BlockSpec(memory_space=pl.ANY), VMEM()],
            out_specs=[VMEM()] * len(turns),
            compiler_params=PARAMS,
            name="gather",
        )(table, after, returned)

    def turn(piece, k):
        return lax.ppermute(piece, "x", [(i, (i + k) % NX) for i in range(NX)])

    far, near = gather((2, 1), sums)
    far, near = turn(far, 2), turn(near, 1)
    sums = add_other(sums, "y", (1, 0, 3, 2))
    last, own = gather((3, 0), sums)
    moved = [own, near, far, turn(last, 3)]
    sums = add_other(sums, "y", (3, 2, 1, 0))
    update = pl.pallas_call(
        finish_kernel,
        out_shape=jax.ShapeDtypeStruct((rows, cols), bf16),
        in_specs=[SMEM()] + [VMEM()] * (NX + 1),
        out_specs=VMEM(),
        compiler_params=PARAMS,
        name="finish",
    )(place.reshape(1, 1), sums, *moved)
    return update, left[None, None], right[None, None]


def solution(mesh):
    wide = Mesh(mesh.devices.reshape(NX, NZ // 2, 2, NT // 2, 2), ("x", "zh", "zl", "y", "c"))
    dp, tensor = ("x", "zh", "zl"), ("y", "c")
    return jax.shard_map(
        body,
        mesh=wide,
        in_specs=(
            P(dp, tensor),
            P(tensor, None, None),
            P(tensor, dp, None, None),
            P(tensor, dp, None, None),
        ),
        out_specs=(P(dp, tensor), P(tensor, dp, None, None), P(tensor, dp, None, None)),
        check_vma=False,
    )
```

```python
import functools

import jax
import jax.numpy as jnp
from jax import lax
from jax.experimental import pallas as pl
from jax.experimental.pallas import tpu as pltpu
from jax.sharding import Mesh
from jax.sharding import PartitionSpec as P

DECAY = 0.9
EPSILON = 1e-06
NX = 4
NZ = 8
NT = 8
COLS = 7
BS = 512
LANES = 128
TILES = BS // LANES
PART = 16
EXTRA = 8
VMEM_LIMIT = 48 * 1024 * 1024

T5 = [3.0517578125, -3.0517578125, 1.220703125, -0.244140625, 0.0244140625, -0.0009765625]
C0 = 25.0 / 16.0
C1 = -5.0 / 16.0 - T5[0] / 4.0
C2, C3, C4, C5, C6 = (-t / 4.0 for t in T5[1:])


def scatter_kernel(owner_ref, rows_ref, out_ref):
    out_ref[...] = jnp.zeros_like(out_ref)
    for i in range(NX):
        for j in range(COLS):
            out_ref[owner_ref[i, j]] = rows_ref[i, :, j * BS : (j + 1) * BS]


def sums_kernel(slots_ref, sums_ref):
    lines = jnp.sum(slots_ref[:, TILES * PART :, :].astype(jnp.float32), axis=0)
    grad = lines[0:1] + (lines[1:2] + lines[2:3])
    cond = lines[3:4] + (lines[4:5] + lines[5:6])
    line = lax.broadcasted_iota(jnp.int32, sums_ref.shape, 0)
    sums_ref[...] = jnp.where(line < 4, grad, cond)


def gather_kernel(turns, owner_ref, after_ref, slots_ref, *out_refs):
    del after_ref
    for k, out_ref in zip(turns, out_refs):
        for j in range(COLS):
            slot = owner_ref[NX + k, j]
            for t in range(TILES):
                out_ref[:, j * BS + t * LANES : j * BS + (t + 1) * LANES] = slots_ref[
                    slot, t * PART : (t + 1) * PART, :
                ]


def finish_kernel(x_ref, sums_ref, *refs):
    scale = jnp.sqrt(sums_ref[0:1, 0:1] / (sums_ref[4:5, 0:1] + EPSILON))
    out_ref = refs[NX]
    for k in range(NX):
        start = pl.multiple_of(((x_ref[0, 0] + NX - k) & (NX - 1)) * PART, PART)
        out_ref[pl.ds(start, PART), :] = (scale * refs[k][...].astype(jnp.float32)).astype(
            jnp.bfloat16
        )


def dot(a, b):
    return jnp.dot(a, b, preferred_element_type=jnp.float32)


def dot_nt(a, b):
    return lax.dot_general(a, b, (((1,), (1,)), ((), ())), preferred_element_type=jnp.float32)


def dot_tn(a, b):
    return lax.dot_general(a, b, (((0,), (0,)), ((), ())), preferred_element_type=jnp.float32)


def split(x):
    high = x.astype(jnp.bfloat16)
    return high, (x - high.astype(jnp.float32)).astype(jnp.bfloat16)


def normalize(stats):
    frob = jnp.sqrt(jnp.sum(stats * stats, keepdims=True) + EPSILON)
    return frob, stats * (1.0 / frob)


def square(n):
    high = n.astype(jnp.bfloat16)
    low2 = (2.0 * (n - high.astype(jnp.float32))).astype(jnp.bfloat16)
    return high, dot(high, high) + dot(high, low2)


def upper_terms(n, n_high, x):
    x_high = x.astype(jnp.bfloat16)
    mixed = n_high * jnp.bfloat16(C5) + x_high * jnp.bfloat16(C6)
    high, low = split(C3 * n + (C4 * x + dot(x_high, mixed)))
    return dot(x_high, high) + dot(x_high, low)


def write_root(root_ref, frob, n, x, upper):
    scale = lax.rsqrt(jnp.sqrt(frob))
    total = (C1 * n + C2 * x) + upper
    root_ref[...] = (total * scale).astype(jnp.bfloat16)
    row = lax.broadcasted_iota(jnp.int32, (LANES, LANES), 0)
    col = lax.broadcasted_iota(jnp.int32, (LANES, LANES), 1)
    constant = jnp.where(row == col, C0, 0.0)
    for t in range(TILES):
        span = slice(t * LANES, (t + 1) * LANES)
        root_ref[span, span] = ((total[span, span] + constant) * scale).astype(jnp.bfloat16)


def slot_at(x, z):
    return (z & 1) * (NX * NZ // 2) + x * (NZ // 2) + (z >> 1)


def refresh_kernel(
    block_ref, left_ref, right_ref, packed_ref, left_out, right_out,
    ordered, left_root, right_root
):
    for p in range(NX):
        for z in range(NZ):
            row = (z * NX + p) * PART
            ordered[row : row + PART, :] = block_ref[p * NZ + z]
    block = ordered[...]
    right = DECAY * right_ref[...] + ((1.0 - DECAY) / BS) * dot_tn(block, block)
    right_out[...] = right
    left = DECAY * left_ref[...] + ((1.0 - DECAY) / BS) * dot_nt(block, block)
    left_out[...] = left
    wide = block.astype(jnp.float32)
    grad_sq = jnp.sum(wide * wide, keepdims=True)
    right_frob, right_n = normalize(right)
    left_frob, left_n = normalize(left)
    right_high, right_x = square(right_n)
    left_high, left_x = square(left_n)
    right_upper = upper_terms(right_n, right_high, right_x)
    left_upper = upper_terms(left_n, left_high, left_x)
    write_root(right_root, right_frob, right_n, right_x, right_upper)
    half = dot(block, right_root[...]).astype(jnp.bfloat16)
    write_root(left_root, left_frob, left_n, left_x, left_upper)
    conditioned = dot(left_root[...], half)
    packed = conditioned.astype(jnp.bfloat16)
    for t in range(TILES):
        tile = packed[:, t * LANES : (t + 1) * LANES].reshape(NZ, NX, PART, LANES)
        for p in range(NX):
            for z in range(NZ):
                packed_ref[slot_at(p, z), t * PART : (t + 1) * PART, :] = tile[z, p]
    line = lax.broadcasted_iota(jnp.int32, (EXTRA, LANES), 0)
    rest = jnp.where(line < 3, grad_sq, jnp.sum(conditioned * conditioned, keepdims=True))
    high = rest.astype(jnp.bfloat16).astype(jnp.float32)
    rest = rest - high
    middle = rest.astype(jnp.bfloat16).astype(jnp.float32)
    low = rest - middle
    kind = jnp.where(line < 3, line, line - 3)
    terms = jnp.where(kind == 0, high, jnp.where(kind == 1, middle, low)).astype(jnp.bfloat16)
    packed_ref[:, TILES * PART :, :] = jnp.broadcast_to(terms[None], (NX * NZ, EXTRA, LANES))


SMEM = functools.partial(pl.BlockSpec, memory_space=pltpu.SMEM)
VMEM = functools.partial(pl.BlockSpec, memory_space=pltpu.VMEM)
PARAMS = pltpu.CompilerParams(vmem_limit_bytes=VMEM_LIMIT)


def add_other(value, axis, partner):
    return value + lax.ppermute(value, axis, list(enumerate(partner)))


def body(gradient, owner, prev_left, prev_right):
    rows, cols = gradient.shape
    part = rows // NX
    place = lax.axis_index("x")
    table = jnp.clip(owner[0], 0, NX * NZ - 1)
    slot = (table & 1) * (NX * NZ // 2) + (table // NZ) * (NZ // 2) + ((table & (NZ - 1)) >> 1)
    table = jnp.concatenate([table, jnp.roll(slot, -place, axis=0)])
    f32, bf16 = jnp.float32, jnp.bfloat16

    spread = lax.all_to_all(gradient.reshape(NX, part, cols), "x", 0, 0, tiled=True)
    slots = pl.pallas_call(
        scatter_kernel,
        out_shape=jax.ShapeDtypeStruct((NX * NZ, part, BS), bf16),
        in_specs=[SMEM(), VMEM()],
        out_specs=VMEM(),
        compiler_params=PARAMS,
        name="scatter",
    )(table, spread)
    block = lax.all_to_all(slots, ("x", "zh", "zl"), 0, 0, tiled=True)

    packed, left, right = pl.pallas_call(
        refresh_kernel,
        out_shape=[
            jax.ShapeDtypeStruct((NX * NZ, TILES * PART + EXTRA, LANES), bf16),
            jax.ShapeDtypeStruct((BS, BS), f32),
            jax.ShapeDtypeStruct((BS, BS), f32),
        ],
        in_specs=[VMEM()] * 3,
        out_specs=[VMEM()] * 3,
        scratch_shapes=[pltpu.VMEM((BS, BS), bf16)] * 3,
        compiler_params=PARAMS,
        name="refresh",
    )(block, prev_left[0, 0], prev_right[0, 0])

    returned = lax.all_to_all(packed, ("zl", "x", "zh"), 0, 0, tiled=True)
    sums = pl.pallas_call(
        sums_kernel,
        out_shape=jax.ShapeDtypeStruct((8, LANES), f32),
        in_specs=[VMEM()],
        out_specs=VMEM(),
        compiler_params=PARAMS,
        name="sums",
    )(returned)
    def gather(turns, after):
        return pl.pallas_call(
            functools.partial(gather_kernel, turns),
            out_shape=[jax.ShapeDtypeStruct((part, cols), bf16)] * len(turns),
            in_specs=[SMEM(), pl.BlockSpec(memory_space=pl.ANY), VMEM()],
            out_specs=[VMEM()] * len(turns),
            compiler_params=PARAMS,
            name="gather",
        )(table, after, returned)

    def turn(piece, k):
        return lax.ppermute(piece, "x", [(i, (i + k) % NX) for i in range(NX)])

    own, near, far, last = gather((0, 1, 2, 3), sums)
    far = turn(far, 2)
    sums = add_other(sums, "c", (1, 0))
    near, sums = lax.optimization_barrier((near, sums))
    near = turn(near, 1)
    sums = add_other(sums, "y", (1, 0, 3, 2))
    last, sums = lax.optimization_barrier((last, sums))
    moved = [own, near, far, turn(last, 3)]
    sums = add_other(sums, "y", (3, 2, 1, 0))
    update = pl.pallas_call(
        finish_kernel,
        out_shape=jax.ShapeDtypeStruct((rows, cols), bf16),
        in_specs=[SMEM()] + [VMEM()] * (NX + 1),
        out_specs=VMEM(),
        compiler_params=PARAMS,
        name="finish",
    )(place.reshape(1, 1), sums, *moved)
    return update, left[None, None], right[None, None]


def solution(mesh):
    wide = Mesh(mesh.devices.reshape(NX, NZ // 2, 2, NT // 2, 2), ("x", "zh", "zl", "y", "c"))
    dp, tensor = ("x", "zh", "zl"), ("y", "c")
    return jax.shard_map(
        body,
        mesh=wide,
        in_specs=(
            P(dp, tensor),
            P(tensor, None, None),
            P(tensor, dp, None, None),
            P(tensor, dp, None, None),
        ),
        out_specs=(P(dp, tensor), P(tensor, dp, None, None), P(tensor, dp, None, None)),
        check_vma=False,
    )
```

```python
import functools

import jax
import jax.numpy as jnp
from jax import lax
from jax.experimental import pallas as pl
from jax.experimental.pallas import tpu as pltpu
from jax.sharding import Mesh
from jax.sharding import PartitionSpec as P

DECAY = 0.9
EPSILON = 1e-06
NX = 4
NZ = 8
NT = 8
COLS = 7
BS = 512
LANES = 128
TILES = BS // LANES
PART = 16
EXTRA = 8
VMEM_LIMIT = 48 * 1024 * 1024

T5 = [3.0517578125, -3.0517578125, 1.220703125, -0.244140625, 0.0244140625, -0.0009765625]
C0 = 25.0 / 16.0
C1 = -5.0 / 16.0 - T5[0] / 4.0
C2, C3, C4, C5, C6 = (-t / 4.0 for t in T5[1:])


def scatter_kernel(owner_ref, rows_ref, out_ref):
    out_ref[...] = jnp.zeros_like(out_ref)
    for i in range(NX):
        for j in range(COLS):
            out_ref[owner_ref[i, j]] = rows_ref[i, :, j * BS : (j + 1) * BS]


def sums_kernel(slots_ref, sums_ref):
    lines = jnp.sum(slots_ref[:, TILES * PART :, :].astype(jnp.float32), axis=0)
    grad = lines[0:1] + (lines[1:2] + lines[2:3])
    cond = lines[3:4] + (lines[4:5] + lines[5:6])
    line = lax.broadcasted_iota(jnp.int32, sums_ref.shape, 0)
    sums_ref[...] = jnp.where(line < 4, grad, cond)


def gather_kernel(turns, owner_ref, after_ref, slots_ref, *out_refs):
    del after_ref
    for k, out_ref in zip(turns, out_refs):
        for j in range(COLS):
            slot = owner_ref[NX + k, j]
            for t in range(TILES):
                out_ref[:, j * BS + t * LANES : j * BS + (t + 1) * LANES] = slots_ref[
                    slot, t * PART : (t + 1) * PART, :
                ]


def finish_kernel(x_ref, sums_ref, *refs):
    scale = jnp.sqrt(sums_ref[0:1, 0:1] / (sums_ref[4:5, 0:1] + EPSILON))
    out_ref = refs[NX]
    for k in range(NX):
        start = pl.multiple_of(((x_ref[0, 0] + NX - k) & (NX - 1)) * PART, PART)
        out_ref[pl.ds(start, PART), :] = (scale * refs[k][...].astype(jnp.float32)).astype(
            jnp.bfloat16
        )


def dot(a, b):
    return jnp.dot(a, b, preferred_element_type=jnp.float32)


def dot_nt(a, b):
    return lax.dot_general(a, b, (((1,), (1,)), ((), ())), preferred_element_type=jnp.float32)


def dot_tn(a, b):
    return lax.dot_general(a, b, (((0,), (0,)), ((), ())), preferred_element_type=jnp.float32)


def split(x):
    high = x.astype(jnp.bfloat16)
    return high, (x - high.astype(jnp.float32)).astype(jnp.bfloat16)


def normalize(stats):
    frob = jnp.sqrt(jnp.sum(stats * stats, keepdims=True) + EPSILON)
    return frob, stats * (1.0 / frob)


def square(n):
    high = n.astype(jnp.bfloat16)
    low2 = (2.0 * (n - high.astype(jnp.float32))).astype(jnp.bfloat16)
    return high, dot(high, high) + dot(high, low2)


def upper_terms(n, n_high, x):
    x_high = x.astype(jnp.bfloat16)
    mixed = n_high * jnp.bfloat16(C5) + x_high * jnp.bfloat16(C6)
    high, low = split(C3 * n + (C4 * x + dot(x_high, mixed)))
    return dot(x_high, high) + dot(x_high, low)


def write_root(root_ref, frob, n, x, upper):
    scale = lax.rsqrt(jnp.sqrt(frob))
    total = (C1 * n + C2 * x) + upper
    root_ref[...] = (total * scale).astype(jnp.bfloat16)
    row = lax.broadcasted_iota(jnp.int32, (LANES, LANES), 0)
    col = lax.broadcasted_iota(jnp.int32, (LANES, LANES), 1)
    constant = jnp.where(row == col, C0, 0.0)
    for t in range(TILES):
        span = slice(t * LANES, (t + 1) * LANES)
        root_ref[span, span] = ((total[span, span] + constant) * scale).astype(jnp.bfloat16)


def slot_at(x, z):
    return (z & 1) * (NX * NZ // 2) + x * (NZ // 2) + (z >> 1)


def refresh_kernel(
    block_ref, left_ref, right_ref, packed_ref, left_out, right_out,
    ordered, left_root, right_root
):
    for p in range(NX):
        for z in range(NZ):
            row = (z * NX + p) * PART
            ordered[row : row + PART, :] = block_ref[slot_at(p, z)]
    block = ordered[...]
    right = DECAY * right_ref[...] + ((1.0 - DECAY) / BS) * dot_tn(block, block)
    right_out[...] = right
    left = DECAY * left_ref[...] + ((1.0 - DECAY) / BS) * dot_nt(block, block)
    left_out[...] = left
    wide = block.astype(jnp.float32)
    grad_sq = jnp.sum(wide * wide, keepdims=True)
    right_frob, right_n = normalize(right)
    left_frob, left_n = normalize(left)
    right_high, right_x = square(right_n)
    left_high, left_x = square(left_n)
    right_upper = upper_terms(right_n, right_high, right_x)
    left_upper = upper_terms(left_n, left_high, left_x)
    write_root(right_root, right_frob, right_n, right_x, right_upper)
    half = dot(block, right_root[...]).astype(jnp.bfloat16)
    write_root(left_root, left_frob, left_n, left_x, left_upper)
    conditioned = dot(left_root[...], half)
    packed = conditioned.astype(jnp.bfloat16)
    for t in range(TILES):
        tile = packed[:, t * LANES : (t + 1) * LANES].reshape(NZ, NX, PART, LANES)
        for p in range(NX):
            for z in range(NZ):
                packed_ref[slot_at(p, z), t * PART : (t + 1) * PART, :] = tile[z, p]
    line = lax.broadcasted_iota(jnp.int32, (EXTRA, LANES), 0)
    rest = jnp.where(line < 3, grad_sq, jnp.sum(conditioned * conditioned, keepdims=True))
    high = rest.astype(jnp.bfloat16).astype(jnp.float32)
    rest = rest - high
    middle = rest.astype(jnp.bfloat16).astype(jnp.float32)
    low = rest - middle
    kind = jnp.where(line < 3, line, line - 3)
    terms = jnp.where(kind == 0, high, jnp.where(kind == 1, middle, low)).astype(jnp.bfloat16)
    packed_ref[:, TILES * PART :, :] = jnp.broadcast_to(terms[None], (NX * NZ, EXTRA, LANES))


SMEM = functools.partial(pl.BlockSpec, memory_space=pltpu.SMEM)
VMEM = functools.partial(pl.BlockSpec, memory_space=pltpu.VMEM)
PARAMS = pltpu.CompilerParams(vmem_limit_bytes=VMEM_LIMIT)


def add_other(value, axis, partner):
    return value + lax.ppermute(value, axis, list(enumerate(partner)))


def body(gradient, owner, prev_left, prev_right):
    rows, cols = gradient.shape
    part = rows // NX
    place = lax.axis_index("x")
    table = jnp.clip(owner[0], 0, NX * NZ - 1)
    slot = (table & 1) * (NX * NZ // 2) + (table // NZ) * (NZ // 2) + ((table & (NZ - 1)) >> 1)
    table = jnp.concatenate([slot, jnp.roll(slot, -place, axis=0)])
    f32, bf16 = jnp.float32, jnp.bfloat16

    spread = lax.all_to_all(gradient.reshape(NX, part, cols), "x", 0, 0, tiled=True)
    slots = pl.pallas_call(
        scatter_kernel,
        out_shape=jax.ShapeDtypeStruct((NX * NZ, part, BS), bf16),
        in_specs=[SMEM(), VMEM()],
        out_specs=VMEM(),
        compiler_params=PARAMS,
        name="scatter",
    )(table, spread)
    block = lax.all_to_all(slots, ("zl", "x", "zh"), 0, 0, tiled=True)

    packed, left, right = pl.pallas_call(
        refresh_kernel,
        out_shape=[
            jax.ShapeDtypeStruct((NX * NZ, TILES * PART + EXTRA, LANES), bf16),
            jax.ShapeDtypeStruct((BS, BS), f32),
            jax.ShapeDtypeStruct((BS, BS), f32),
        ],
        in_specs=[VMEM()] * 3,
        out_specs=[VMEM()] * 3,
        scratch_shapes=[pltpu.VMEM((BS, BS), bf16)] * 3,
        compiler_params=PARAMS,
        name="refresh",
    )(block, prev_left[0, 0], prev_right[0, 0])

    returned = lax.all_to_all(packed, ("zl", "x", "zh"), 0, 0, tiled=True)
    sums = pl.pallas_call(
        sums_kernel,
        out_shape=jax.ShapeDtypeStruct((8, LANES), f32),
        in_specs=[VMEM()],
        out_specs=VMEM(),
        compiler_params=PARAMS,
        name="sums",
    )(returned)
    def gather(turns, after):
        return pl.pallas_call(
            functools.partial(gather_kernel, turns),
            out_shape=[jax.ShapeDtypeStruct((part, cols), bf16)] * len(turns),
            in_specs=[SMEM(), pl.BlockSpec(memory_space=pl.ANY), VMEM()],
            out_specs=[VMEM()] * len(turns),
            compiler_params=PARAMS,
            name="gather",
        )(table, after, returned)

    def turn(piece, k):
        return lax.ppermute(piece, "x", [(i, (i + k) % NX) for i in range(NX)])

    own, near, far, last = gather((0, 1, 2, 3), sums)
    far = turn(far, 2)
    sums = add_other(sums, "c", (1, 0))
    near, sums = lax.optimization_barrier((near, sums))
    near = turn(near, 1)
    sums = add_other(sums, "y", (1, 0, 3, 2))
    last, sums = lax.optimization_barrier((last, sums))
    moved = [own, near, far, turn(last, 3)]
    sums = add_other(sums, "y", (3, 2, 1, 0))
    update = pl.pallas_call(
        finish_kernel,
        out_shape=jax.ShapeDtypeStruct((rows, cols), bf16),
        in_specs=[SMEM()] + [VMEM()] * (NX + 1),
        out_specs=VMEM(),
        compiler_params=PARAMS,
        name="finish",
    )(place.reshape(1, 1), sums, *moved)
    return update, left[None, None], right[None, None]


def solution(mesh):
    wide = Mesh(mesh.devices.reshape(NX, NZ // 2, 2, NT // 2, 2), ("x", "zh", "zl", "y", "c"))
    dp, tensor = ("x", "zh", "zl"), ("y", "c")
    return jax.shard_map(
        body,
        mesh=wide,
        in_specs=(
            P(dp, tensor),
            P(tensor, None, None),
            P(tensor, dp, None, None),
            P(tensor, dp, None, None),
        ),
        out_specs=(P(dp, tensor), P(tensor, dp, None, None), P(tensor, dp, None, None)),
        check_vma=False,
    )
```
